256 devices in a mesh: dp: 8 (over z_hi, y), pipe: 4 (over x), tensor: 8 (over z_lo, core).
Axes of the slice: x: 4, y: 4, z: 8 (z_hi: 2, z_lo: 4; z = z_hi * 4 + z_lo), core: 2. Of those that a mesh axis runs over, the one named last changes fastest.
Arguments:
- emb: bfloat16 [25600, 12288], P('tensor', 'dp'), may hold values from -0.17140086 to 0.17140086
- final_hidden: bfloat16 [192, 12288], P(None, 'dp'), may hold values from -8 to 8
- section_inputs: bfloat16 [4, 192, 12288], P('pipe', None, 'dp'), may hold values from -6 to 6
- gains: float32 [4, 12288], P('pipe', 'dp'), may hold values from 0.1 to 1.9
- token_ids: int32 [192], replicated, may hold values from 0 to 25599
- targets: int32 [192], replicated, may hold values from 0 to 25599
Outputs:
- emb_grad: bfloat16 [25600, 12288], P('tensor', ('dp', 'pipe'))
The draws below stay inside these ranges and needn't reach their ends.
All inputs are finite; a program needn't handle non-finite values.
Results may differ from the reference program's by a relative error of at most 0.0067.
Values may be sent and summed in bfloat16 or wider, within the bound.
A program may use at most 128 MiB of HBM per device.

```python
import math
import jax
import jax.numpy as jnp
import numpy as np
from jax import lax

D = 12288
VOCAB = 25600
TOKENS = 192
SECTIONS = 4


def embed_base(key):
    return jnp.clip(jax.random.normal(key, (VOCAB, D), jnp.float32), -6.0, 6.0)


def draw_emb(key, part):
    base = embed_base(key)
    return (base * (3.0 / math.sqrt(D))).astype(jnp.bfloat16)


def draw_final_hidden(key, part):
    key = jax.random.fold_in(key, 23)
    keys = jax.random.split(key, 3)
    values = jax.random.normal(keys[2], (TOKENS, D), jnp.float32)
    return jnp.clip(values, -6.0, 6.0).astype(jnp.bfloat16)


def draw_section_inputs(key, part):
    key = jax.random.fold_in(key, 37)
    keys = jax.random.split(key, 5)
    column = jnp.arange(D).astype(jnp.float32) / D
    rise = jnp.exp(math.log(3.0) * column)[None, None, :]
    rough = jnp.exp(jax.random.uniform(keys[0], (SECTIONS, 1, D), jnp.float32, 0.0, math.log(3.0)))
    offset = 0.3 * jax.random.normal(keys[1], (SECTIONS, TOKENS, 1), jnp.float32)
    values = 0.15 * jax.random.normal(keys[4], (SECTIONS, TOKENS, D), jnp.float32)
    return jnp.clip(values * rise * rough + offset, -6.0, 6.0).astype(jnp.bfloat16)


def touch_ends(array, rng, low, top_value):
    index_at = [jax.random.randint(jax.random.fold_in(rng, axis), (), 0, length) for axis, length in enumerate(array.shape)]
    longest = array.shape.index(max(array.shape))
    neighbour = index_at[:longest] + [(index_at[longest] + 1) % array.shape[longest]] + index_at[longest + 1:]
    return array.at[tuple(index_at)].set(low).at[tuple(neighbour)].set(top_value)


def rank_table(number_of, lean):
    loads = [(1 << 20) // math.isqrt(standing ** lean) + 1 for standing in range(1, number_of + 1)]
    spread = 1 + sum(loads) // (1 << 30)
    return np.cumsum(np.array([max(1, weight // spread) for weight in loads]))


def skewed_ids(key, dims, number_of, skew):
    grid = rank_table(number_of, skew)
    lot = jax.random.randint(jax.random.fold_in(key, 1), dims, 0, int(grid[number_of - 1]))
    standing = jnp.searchsorted(jnp.asarray(grid, jnp.int32), lot, side="right")
    return jax.random.permutation(jax.random.fold_in(key, 2), number_of)[standing].astype(jnp.int32)


def setup_inputs(seed: int = 0) -> dict:
    seeds = jax.random.split(jax.random.key(seed), 7)
    emb = draw_emb(jax.random.fold_in(seeds[6], 71), 0)
    final_hidden = draw_final_hidden(jax.random.fold_in(seeds[6], 71), 0)
    section_inputs = draw_section_inputs(jax.random.fold_in(seeds[6], 71), 0)
    gains = jnp.clip(1.0 + 0.18 * jax.random.normal(seeds[3], (SECTIONS, D), jnp.float32), 0.1, 1.9)
    token_ids = touch_ends(skewed_ids(seeds[4], (TOKENS,), VOCAB, 2), jax.random.fold_in(seeds[4], 3), 0, VOCAB - 1).astype(jnp.int32)
    targets = touch_ends(skewed_ids(seeds[5], (TOKENS,), VOCAB, 2), jax.random.fold_in(seeds[5], 3), 0, VOCAB - 1).astype(jnp.int32)
    return dict(emb=emb, final_hidden=final_hidden, section_inputs=section_inputs, gains=gains, token_ids=token_ids, targets=targets)


eps = 1e-05

def reference(emb, final_hidden, section_inputs, gains, token_ids, targets):
    logits = jnp.dot(final_hidden, emb.T, preferred_element_type=jnp.float32)
    row_top = lax.optimization_barrier(jnp.max(logits, axis=1, keepdims=True))
    expo = jnp.exp(logits - row_top)
    probs = expo / lax.optimization_barrier(jnp.sum(expo, axis=1, keepdims=True))
    vocab_index = lax.broadcasted_iota(jnp.int32, logits.shape, 1)
    onehot = (vocab_index == targets[:, None]).astype(jnp.float32)
    logit_grad = (probs - onehot).astype(jnp.bfloat16)
    gradient = jnp.dot(logit_grad, emb, preferred_element_type=jnp.float32).astype(jnp.bfloat16)
    for section in range(SECTIONS - 1, -1, -1):
        saved = section_inputs[section].astype(jnp.float32)
        mean_x = lax.optimization_barrier(jnp.mean(saved, axis=1))
        rstd = 1.0 / jnp.sqrt(lax.optimization_barrier(jnp.mean(saved * saved, axis=1)) - mean_x * mean_x + eps)
        normed = (saved - mean_x[:, None]) * rstd[:, None]
        scaled = gradient.astype(jnp.float32) * gains[section][None, :]
        first_mean = lax.optimization_barrier(jnp.mean(scaled, axis=1, keepdims=True))
        second_mean = lax.optimization_barrier(jnp.mean(scaled * normed, axis=1, keepdims=True))
        delta = rstd[:, None] * (scaled - first_mean - normed * second_mean)
        gradient = (gradient.astype(jnp.float32) + delta).astype(jnp.bfloat16)
    head_grad = jnp.dot(logit_grad.T, final_hidden, preferred_element_type=jnp.float32).astype(jnp.bfloat16)
    input_grad = jax.ops.segment_sum(gradient.astype(jnp.float32), token_ids.astype(jnp.int32), VOCAB).astype(jnp.bfloat16)
    return (head_grad.astype(jnp.float32) + input_grad.astype(jnp.float32)).astype(jnp.bfloat16)
```

```python
import functools

import jax
import jax.numpy as jnp
from jax import lax
from jax.experimental import pallas as pl
from jax.experimental.pallas import tpu as pltpu
from jax.sharding import PartitionSpec as P

eps = 1e-05
f32 = jnp.float32
bf16 = jnp.bfloat16
MESH = pl.DeviceIdType.MESH
LOW = -3.0e38

T, V, C = 192, 3200, 1536
D = 12288
W = 896
Q = 384
B = 48
H = 96
R = 24
N_SEM = 128


def iota(shape, axis):
    return lax.broadcasted_iota(jnp.int32, shape, axis)


def pick_rows(rows, count):
    index = iota((count, 128), 0)
    out = jnp.zeros((count, 128), f32)
    for i, row in enumerate(rows):
        out = jnp.where(index == i, jnp.broadcast_to(row, (count, 128)), out)
    return out


def to_rows(cols, count):
    n = cols[0].shape[0]
    lane = iota((n, 128), 1)
    out = jnp.zeros((n, 128), f32)
    for i, col in enumerate(cols):
        out = jnp.where(lane == i, col, out)
    out = jnp.concatenate([out, jnp.zeros((128 - n, 128), f32)], axis=0)
    return out.T[:count]


def to_cols(tile):
    r = tile.shape[0]
    return jnp.concatenate([tile, jnp.zeros((128 - r, 128), f32)], axis=0).T


def kernel(
    emb, fh_h, x_h, gains_h, tgt_h, hd_out, g0_out,
    ew, ec, fh, xv, gv, tv, tcol, gb,
    lp, ly, zl_buf, zr_buf, pb,
    st, st2, sc,
    xt, xsl, xz, xs, gs, cs, rr, xhs,
    gt, gx, gt2, gy, gt3, gz, gram,
    G, cr, gh, zrs, ga, sm, smz, sm2, smxy, g0f, g0b, hd,
    lsem, ss, rs,
):
    d = lax.axis_index("dp")
    px = lax.axis_index("pipe")
    t = lax.axis_index("tensor")
    y, zh = d % 4, d // 4
    zl, c = t // 2, t % 2
    z = zh * 4 + zl

    def at(x_=None, y_=None, z_=None, c_=None):
        x_ = px if x_ is None else x_
        y_ = y if y_ is None else y_
        z_ = z if z_ is None else z_
        c_ = c if c_ is None else c_
        return ((z_ // 4) * 4 + y_, x_, (z_ % 4) * 2 + c_)

    def xy(i):
        return at(x_=(px + i // 4) % 4, y_=(y + i % 4) % 4)

    def zring(k):
        return at(z_=(z + k) % 8)

    def zline(k):
        return zh * 4 + (zl + k) % 4

    used = [0]

    def sems(n):
        used[0] += n
        assert used[0] <= N_SEM
        return used[0] - n

    def rc(src, dst, i, dev):
        return pltpu.make_async_remote_copy(
            src_ref=src, dst_ref=dst, send_sem=ss.at[i], recv_sem=rs.at[i],
            device_id=dev, device_id_type=MESH,
        )

    pending = []

    def send(cp):
        cp.start()
        pending.append(cp)
        return cp

    mult = pl.multiple_of
    my_tok = pl.ds(mult(c * H, 16), H)
    other_tok = pl.ds(mult((1 - c) * H, 16), H)

    loads = [
        pltpu.make_async_copy(x_h.at[0], xv, lsem.at[0]),
        pltpu.make_async_copy(gains_h, gv, lsem.at[1]),
        pltpu.make_async_copy(tgt_h, tv, lsem.at[2]),
        pltpu.make_async_copy(fh_h, fh, lsem.at[3]),
        pltpu.make_async_copy(emb.at[pl.ds(mult(px * 768, 128), W), :], ew, lsem.at[4]),
        pltpu.make_async_copy(emb.at[:, pl.ds(mult(px * Q, 128), Q)], ec, lsem.at[5]),
    ]
    for cp in loads:
        cp.start()
    bar = pltpu.get_barrier_semaphore()

    @pl.loop(1, 16)
    def _(i):
        pl.semaphore_signal(bar, inc=1, device_id=xy(i), device_id_type=MESH)

    for k in range(1, 8):
        pl.semaphore_signal(bar, inc=1, device_id=zring(k), device_id_type=MESH)
    for k in range(4):
        pl.semaphore_signal(bar, inc=1, device_id=at(z_=zline(k), c_=1 - c), device_id_type=MESH)

    loads[0].wait()
    xf = xv[my_tok, :].astype(f32)
    xt[...] = to_rows([jnp.sum(xf, axis=1, keepdims=True), jnp.sum(xf * xf, axis=1, keepdims=True)], 8)
    loads[1].wait()
    gb[...] = jnp.broadcast_to(gv[...], (8, C))
    loads[2].wait()
    tcol[...] = jnp.sum(
        jnp.where(iota((T, T), 0) == iota((T, T), 1), tv[...].astype(f32), 0.0), axis=1, keepdims=True
    ).astype(jnp.int32)

    loads[3].wait()
    loads[4].wait()

    @pl.loop(0, 7)
    def _(i):
        tile = pl.ds(mult(i * 128, 128), 128)
        lp[:, tile] = lax.dot_general(
            fh[...], ew[tile, :], (((1,), (1,)), ((), ())), preferred_element_type=f32
        )

    pl.semaphore_wait(bar, 26)

    sy = sems(3)
    ycp = []
    for k in (1, 3, 2):
        to = (y + k) % 4
        ycp.append(send(rc(lp.at[pl.ds(mult(to * B, 16), B), :], ly.at[k - 1], sy + k - 1, at(y_=to))))

    sx = sems(3)
    sg = sems(3)
    for k in range(1, 4):
        to = (px + k) % 4
        cols = pl.ds(mult(to * Q, 128), Q)
        send(rc(xv.at[my_tok, cols], xs.at[px], sx + k - 1, at(x_=to)))
        send(rc(gb.at[:, cols], gs.at[px], sg + k - 1, at(x_=to)))
    my_cols = pl.ds(mult(px * Q, 128), Q)
    xs[px] = xv[my_tok, my_cols]
    gs[px] = gb[:, my_cols]
    s1 = sems(16)
    xsl[px * 4 + y] = xt[...]

    @pl.loop(1, 16)
    def _(i):
        rc(xt, xsl.at[px * 4 + y], s1 + i, xy(i)).start()

    @pl.loop(1, 16)
    def _(i):
        slot = ((px - i // 4 + 4) % 4) * 4 + (y - i % 4 + 4) % 4
        rc(xt, xsl.at[slot], s1 + i, xy(i)).wait_recv()

    rows = []
    for s in range(4):
        tot = xsl[4 * s] + xsl[4 * s + 1] + xsl[4 * s + 2] + xsl[4 * s + 3]
        rows += [tot[0:1], tot[1:2]]
    xz[0] = pick_rows(rows, 8)
    s2 = sems(1)
    xzcp = send(rc(xz.at[0], xz.at[1], s2, zring(4)))

    for cp in ycp:
        cp.wait_recv()
    zl_buf[...] = lp[pl.ds(mult(y * B, 16), B), :] + ly[0] + ly[1] + ly[2]
    sz = sems(1)
    zcp = send(rc(zl_buf, zr_buf, sz, zring(4)))

    xzcp.wait_recv()
    tot = (xz[0] + xz[1]) * (1.0 / D)
    mu_rows, r_rows = [], []
    for s in range(4):
        mu = tot[2 * s : 2 * s + 1]
        mu_rows.append(mu)
        r_rows.append(lax.rsqrt(tot[2 * s + 1 : 2 * s + 2] - mu * mu + eps))
    rr[...] = pick_rows(r_rows, 8)
    cs[...] = to_cols(pick_rows(mu_rows + r_rows, 8))
    for k in range(1, 4):
        src = (px - k + 4) % 4
        rc(xv.at[my_tok, my_cols], xs.at[src], sx + k - 1, at(x_=src)).wait_recv()
        rc(gb.at[:, my_cols], gs.at[src], sg + k - 1, at(x_=src)).wait_recv()
    for s in range(4):
        xhs[s] = (xs[s].astype(f32) - cs[0:H, s : s + 1]) * cs[0:H, 4 + s : 5 + s]

    def gain(s):
        return gs[s][0:1, :]

    def rsum(v):
        return jnp.sum(v, axis=1, keepdims=True)

    cols = []
    for j in range(1, 4):
        q1 = jnp.ones((H, Q), f32)
        q2 = xhs[j]
        for s in range(j - 1, -1, -1):
            a1 = q1 * gain(s)
            a2 = q2 * gain(s)
            xh = xhs[s]
            cols += [rsum(a1), rsum(a1 * xh), rsum(a2), rsum(a2 * xh)]
            if s > 0:
                r_col = cs[0:H, 4 + s : 5 + s]
                q1 = q1 + r_col * a1
                q2 = q2 + r_col * a2
    gt[...] = to_rows(cols, 24)
    sgx = sems(3)
    gxcp = [send(rc(gt, gx.at[k - 1], sgx + k - 1, at(x_=(px + k) % 4))) for k in range(1, 4)]

    zcp.wait_recv()
    my_rows = pl.ds(mult(y * B, 16), B)
    lane = iota((B, W), 1)
    valid = lane >= jnp.where(px == 0, 0, 128)
    logits = jnp.where(valid, zl_buf[...] + zr_buf[...], LOW)
    m = jnp.max(logits, axis=1, keepdims=True)
    e = jnp.where(valid, jnp.exp(logits - m), 0.0)
    hit = (lane + (t * V + px * 768) == tcol[my_rows, :]) & valid
    tl = rsum(jnp.where(hit, logits, 0.0))
    pb[px, my_rows, :] = e.astype(bf16)
    st[0] = to_rows([m, rsum(e), tl], 8)

    def peer1(k):
        return at(x_=(px + k * c) % 4, y_=(y + k * (1 - c)) % 4)

    def peer2(k):
        return at(x_=(px + k * (1 - c)) % 4, y_=(y + k * c) % 4)

    def block(b, e_):
        bx = (px - b * c - e_ * (1 - c) + 4) % 4
        by = (y - b * (1 - c) - e_ * c + 4) % 4
        return bx, by

    def pref(b, e_):
        bx, by = block(b, e_)
        return pb.at[bx, pl.ds(mult(by * B, 16), B), :]

    a1 = sems(3)
    a2 = sems(12)
    sst = sems(8)
    for k in (1, 3, 2):
        send(rc(pref(0, 0), pref(0, 0), a1 + k - 1, peer1(k)))
    stcp = []
    for k in range(1, 8):
        stcp.append(send(rc(st.at[0], st.at[k], sst + k, at(z_=zline(k // 2), c_=(c + k % 2) % 2))))
    for k in (1, 3, 2):
        send(rc(pref(0, 0), pref(0, 0), a2 + k - 1, peer2(k)))

    for cp in gxcp:
        cp.wait_recv()
    gt2[...] = gt[...] + gx[0] + gx[1] + gx[2]
    sgy = sems(3)
    gycp = [send(rc(gt2, gy.at[k - 1], sgy + k - 1, at(y_=(y + k) % 4))) for k in range(1, 4)]

    for cp in stcp:
        cp.wait_recv()
    tiles = [st[k] for k in range(8)]
    top = functools.reduce(jnp.maximum, [a[0:1] for a in tiles])
    total = sum(a[1:2] * jnp.exp(a[0:1] - top) for a in tiles)
    hitsum = sum(a[2:3] for a in tiles)
    mine = px * 4 + y
    st2[mine] = pick_rows([top, total, hitsum, tiles[0][0:1]], 8)
    s3 = sems(16)

    @pl.loop(1, 16)
    def _(i):
        rc(st2.at[mine], st2.at[mine], s3 + i, xy(i)).start()

    for b in (1, 3, 2):
        rc(pref(0, 0), pref(b, 0), a1 + b - 1, peer1(b)).wait_recv()
        for k in (1, 3, 2):
            send(rc(pref(b, 0), pref(b, 0), a2 + 3 * b + k - 1, peer2(k)))

    for cp in gycp:
        cp.wait_recv()
    gt3[...] = gt2[...] + gy[0] + gy[1] + gy[2]
    sgz = sems(1)
    gzcp = send(rc(gt3, gz, sgz, zring(4)))

    @pl.loop(1, 16)
    def _(i):
        slot = ((px - i // 4 + 4) % 4) * 4 + (y - i % 4 + 4) % 4
        rc(st2.at[mine], st2.at[slot], s3 + i, xy(i)).wait_recv()

    rows = []
    for yy in range(4):
        tiles = [st2[4 * xx + yy] for xx in range(4)]
        top = functools.reduce(jnp.maximum, [a[0:1] for a in tiles])
        total = sum(a[1:2] * jnp.exp(a[0:1] - top) for a in tiles)
        inv = 1.0 / total
        rows += [jnp.exp(a[3:4] - top) * inv for a in tiles]
        rows += [jnp.exp(sum(a[2:3] for a in tiles) - top) * inv - 1.0]
        rows += [jnp.zeros((1, 128), f32)] * 3
    sc[...] = to_cols(pick_rows(rows, 32))

    def normalise(b, e_):
        bx, by = block(b, e_)
        blk = pl.ds(mult(by * B, 16), B)
        scale = rsum(jnp.where(iota((B, 128), 1) == by * 8 + bx, sc[0:B, :], 0.0))
        point = rsum(jnp.where(iota((B, 128), 1) == by * 8 + 4, sc[0:B, :], 0.0))
        hit = (lane + (t * V + bx * 768) == tcol[blk, :]) & (lane >= jnp.where(bx == 0, 0, 128))
        pb[bx, blk, :] = jnp.where(hit, point, pb[bx, blk, :].astype(f32) * scale).astype(bf16)

    for cp in pending:
        cp.wait_send()
    pending.clear()

    @pl.loop(0, 4)
    def _(b):
        normalise(b, 0)

    for b in (0, 1, 3, 2):
        for k in (1, 3, 2):
            rc(pref(0, 0), pref(b, k), a2 + 3 * b + k - 1, peer2(k)).wait_recv()
            normalise(b, k)

    loads[5].wait()
    G[...] = jnp.dot(pb[0], ec[0:W, :], preferred_element_type=f32)

    @pl.loop(1, 4)
    def _(i):
        G[...] += jnp.dot(pb[i], ec[pl.ds(mult(i * 768, 128), W), :], preferred_element_type=f32)

    sc0 = sems(1)
    corecp = send(rc(G.at[other_tok, :], cr, sc0, at(c_=1 - c)))
    gzcp.wait_recv()
    gram[...] = gt3[...] + gz[...]
    corecp.wait_recv()
    gh[...] = G[my_tok, :] + cr[...]
    szr = sems(3)
    zrcp = []
    for k in (1, 3, 2):
        to = (zl + k) % 4
        zrcp.append(send(rc(gh.at[pl.ds(mult(to * R, 8), R), :], zrs.at[k - 1], szr + k - 1, at(z_=zline(k)))))

    q = gh[...]
    cols = []
    for s in (3, 2, 1, 0):
        a = q * gain(s)
        cols += [rsum(a), rsum(a * xhs[s])]
        if s > 0:
            q = q + cs[0:H, 4 + s : 5 + s] * a
    sm[...] = to_rows(cols, 8)
    ssm = sems(8)
    smcp = [send(rc(sm, smz.at[k], ssm + k, zring(k))) for k in range(1, 8)]

    fcols = fh[:, my_cols]

    def head(lo, hi):
        @pl.loop(lo, hi)
        def _(i):
            xx = jnp.maximum(i - 1, 0) // 6
            loc = i - 6 * xx
            out = lax.dot_general(
                pb[xx, :, pl.ds(mult(loc * 128, 128), 128)], fcols,
                (((0,), (0,)), ((), ())), preferred_element_type=f32,
            )
            hd[pl.ds(mult(i * 128, 128), 128), :] = out.astype(bf16)

    head(0, 12)

    for cp in zrcp:
        cp.wait_recv()
    mine24 = gh[pl.ds(mult(zl * R, 8), R), :] + zrs[0] + zrs[1] + zrs[2]
    ga[zl] = jnp.concatenate([mine24, jnp.zeros((8, Q), f32)], axis=0).astype(bf16)
    sga = sems(3)
    for k in (1, 3, 2):
        send(rc(ga.at[zl], ga.at[zl], sga + k - 1, at(z_=zline(k))))

    for cp in smcp:
        cp.wait_recv()
    sm2[...] = sm[...] + sum(smz[k] for k in range(1, 8))
    sxy = sems(16)

    @pl.loop(1, 16)
    def _(i):
        rc(sm2, smxy.at[i], sxy + i, xy(i)).start()

    head(12, 25)
    hdcp = pltpu.make_async_copy(hd, hd_out, lsem.at[6])
    hdcp.start()

    @pl.loop(1, 16)
    def _(i):
        rc(sm2, smxy.at[i], sxy + i, xy(i)).wait_recv()

    sums = (sm2[...] + sum(smxy[i] for i in range(1, 16))) * (1.0 / D)
    gram_m = gram[...] * (1.0 / D)
    base = {}
    for j in range(1, 4):
        for s in range(j - 1, -1, -1):
            base[j, s] = 4 * len(base)
    c1, c2 = {}, {}
    for n, s in enumerate((3, 2, 1, 0)):
        m1 = sums[2 * n : 2 * n + 1]
        m2 = sums[2 * n + 1 : 2 * n + 2]
        for j in range(s + 1, 4):
            o = base[j, s]
            m1 = m1 - c1[j] * gram_m[o : o + 1] - c2[j] * gram_m[o + 2 : o + 3]
            m2 = m2 - c1[j] * gram_m[o + 1 : o + 2] - c2[j] * gram_m[o + 3 : o + 4]
        c1[s] = rr[s : s + 1, :] * m1
        c2[s] = rr[s : s + 1, :] * m2
    coef = to_cols(pick_rows([c1[s] for s in range(4)] + [c2[s] for s in range(4)], 8))

    for k in range(1, 4):
        src = (zl - k + 4) % 4
        rc(ga.at[zl], ga.at[src], sga + k - 1, at(z_=zline(k))).wait_recv()
    for zz in range(4):
        g0f[R * zz : R * zz + R, :] = ga[zz].astype(f32)[0:R]
    h = g0f[...]
    for s in (3, 2, 1, 0):
        h = h + cs[0:H, 4 + s : 5 + s] * (h * gain(s)) - coef[0:H, s : s + 1] - coef[0:H, 4 + s : 5 + s] * xhs[s]
    g0b[my_tok, :] = h.astype(bf16)
    sc1 = sems(1)
    g0cp = send(rc(g0b.at[my_tok, :], g0b.at[my_tok, :], sc1, at(c_=1 - c)))
    rc(g0b.at[my_tok, :], g0b.at[other_tok, :], sc1, at(c_=1 - c)).wait_recv()
    g0_out[...] = g0b[...]

    for cp in pending:
        cp.wait_send()

    @pl.loop(1, 16)
    def _(i):
        rc(xt, xsl.at[0], s1 + i, xy(i)).wait_send()
        rc(st2.at[mine], st2.at[mine], s3 + i, xy(i)).wait_send()
        rc(sm2, smxy.at[i], sxy + i, xy(i)).wait_send()

    hdcp.wait()


def add_rows(hd, g0, ids, out):
    first = lax.axis_index("tensor") * V + pl.program_id(0) * out.shape[0]
    rows = iota((out.shape[0], T), 0) + first
    onehot = (rows == ids[...]).astype(f32).astype(bf16)
    added = jnp.dot(onehot, g0[...], preferred_element_type=f32).astype(bf16)
    out[...] = (hd[...].astype(f32) + added.astype(f32)).astype(bf16)


def local(emb, final_hidden, section_inputs, gains, token_ids, targets):
    any_ = pl.BlockSpec(memory_space=pl.ANY)
    vm = lambda shape, dtype=f32: pltpu.VMEM(shape, dtype)
    tile = (8, 128)
    hd, g0 = pl.pallas_call(
        kernel,
        out_shape=(jax.ShapeDtypeStruct((V, Q), bf16), jax.ShapeDtypeStruct((T, Q), bf16)),
        in_specs=[any_] * 5,
        out_specs=(any_, pl.BlockSpec(memory_space=pltpu.VMEM)),
        scratch_shapes=[
            vm((W, C), bf16), vm((V, Q), bf16), vm((T, C), bf16), vm((T, C), bf16),
            vm((1, C)), vm((1, T), jnp.int32), vm((T, 1), jnp.int32), vm((8, C)),
            vm((T, W)), vm((3, B, W)), vm((B, W)), vm((B, W)), vm((4, T, W), bf16),
            vm((8,) + tile), vm((16,) + tile), vm((128, 128)),
            vm(tile), vm((16,) + tile), vm((2,) + tile), vm((4, H, Q), bf16), vm((4, 8, Q)),
            vm((128, 128)), vm(tile), vm((4, H, Q)),
            vm((24, 128)), vm((3, 24, 128)), vm((24, 128)), vm((3, 24, 128)),
            vm((24, 128)), vm((24, 128)), vm((24, 128)),
            vm((T, Q)), vm((H, Q)), vm((H, Q)), vm((3, R, Q)), vm((4, 32, Q), bf16),
            vm(tile), vm((8,) + tile), vm(tile), vm((16,) + tile), vm((H, Q)), vm((T, Q), bf16),
            vm((V, Q), bf16),
            pltpu.SemaphoreType.DMA((7,)),
            pltpu.SemaphoreType.DMA((N_SEM,)), pltpu.SemaphoreType.DMA((N_SEM,)),
        ],
        name="relay",
        compiler_params=pltpu.CompilerParams(
            collective_id=0, has_side_effects=True, vmem_limit_bytes=40 * 2**20
        ),
    )(emb, final_hidden, section_inputs, gains, targets.reshape(1, T))
    step = 640
    return pl.pallas_call(
        add_rows,
        grid=(V // step,),
        out_shape=jax.ShapeDtypeStruct((V, Q), bf16),
        in_specs=[
            pl.BlockSpec((step, Q), lambda i: (i, 0)),
            pl.BlockSpec((T, Q), lambda i: (0, 0)),
            pl.BlockSpec((1, T), lambda i: (0, 0)),
        ],
        out_specs=pl.BlockSpec((step, Q), lambda i: (i, 0)),
        name="add_rows",
    )(hd, g0, token_ids.reshape(1, T))


def solution(mesh):
    placed = (P("tensor", "dp"), P(None, "dp"), P("pipe", None, "dp"), P("pipe", "dp"), P(), P())
    return jax.shard_map(
        local, mesh=mesh, in_specs=placed, out_specs=P("tensor", ("dp", "pipe")), check_vma=False
    )
```

```python
import functools

import jax
import jax.numpy as jnp
from jax import lax
from jax.experimental import pallas as pl
from jax.experimental.pallas import tpu as pltpu
from jax.sharding import PartitionSpec as P

eps = 1e-05
f32 = jnp.float32
bf16 = jnp.bfloat16
MESH = pl.DeviceIdType.MESH
LOW = -3.0e38

T, V, C = 192, 3200, 1536
D = 12288
W = 896
Q = 384
B = 48
H = 96
R = 24
N_SEM = 48
CHUNKS = ((0, 512), (512, 384))
STEP = 640


def iota(shape, axis):
    return lax.broadcasted_iota(jnp.int32, shape, axis)


def pick_rows(rows, count):
    index = iota((8, 128), 0)
    tiles = []
    for start in range(0, count, 8):
        out = jnp.zeros((8, 128), f32)
        for i, row in enumerate(rows[start : start + 8]):
            if row is not None:
                out = jnp.where(index == i, jnp.broadcast_to(row, (8, 128)), out)
        tiles.append(out)
    return tiles[0] if len(tiles) == 1 else jnp.concatenate(tiles, axis=0)


def to_rows(cols, count):
    n = cols[0].shape[0]
    lane = iota((n, 128), 1)
    out = jnp.zeros((n, 128), f32)
    for i, col in enumerate(cols):
        out = jnp.where(lane == i, col, out)
    out = jnp.concatenate([out, jnp.zeros((128 - n, 128), f32)], axis=0)
    return out.T[:count]


def rsum(v):
    return jnp.sum(v, axis=1, keepdims=True)


def to_cols(tile):
    r = tile.shape[0]
    if r < 128:
        tile = jnp.concatenate([tile, jnp.zeros((128 - r, 128), f32)], axis=0)
    return tile.T


def kernel(
    emb, fh_h, x_h, gains_h, tgt_h, hd, g0b,
    ew, ec, fh, xv, gv, tv, tcol, gb,
    lp, ly, zl_buf, zr_buf, pb, pn,
    st, st2, sc,
    xt, xsl, xz, xs, gs, cs, rr, xhs,
    gt, gx, gt2, gy, gt3, gz, gram,
    G, cr, gh, zrs, ga, sm, smz, sm2, smxy, g0f, g0s,
    lsem, ss, rs,
):
    d = lax.axis_index("dp")
    px = lax.axis_index("pipe")
    t = lax.axis_index("tensor")
    y, zh = lax.rem(d, 4), lax.div(d, 4)
    zl, c = lax.rem(lax.div(t, 2), 4), lax.rem(t, 2)
    z = zh * 4 + zl
    oc = 1 - c
    xs_at = [lax.rem(px + k, 4) for k in range(4)]
    ys_at = [lax.rem(y + k, 4) for k in range(4)]
    zl_at = [lax.rem(zl + k, 4) for k in range(4)]
    zr_at = [lax.rem(z + k, 8) for k in range(8)]
    base = d - y
    plane = [(base + ys_at[j], xs_at[i], t) for i in range(4) for j in range(4)]
    ring = [(lax.div(zz, 4) * 4 + y, px, lax.rem(zz, 4) * 2 + c) for zz in zr_at]
    group = [(d, px, zl_at[k // 2] * 2 + (oc if k % 2 else c)) for k in range(8)]
    line = [group[2 * k] for k in range(4)]
    twin = group[1]

    used = [0]

    def sems(n):
        used[0] += n
        assert used[0] <= N_SEM
        return used[0] - n

    sent = []

    def send(src, dst, i, dev):
        pltpu.make_async_remote_copy(
            src_ref=src, dst_ref=dst, send_sem=ss.at[i], recv_sem=rs.at[i],
            device_id=dev, device_id_type=MESH,
        ).start()

    def landed(ref, i):
        pltpu.make_async_copy(ref, ref, rs.at[i]).wait()
        sent.append((ref, i))

    def flush():
        for ref, i in sent:
            pltpu.make_async_copy(ref, ref, ss.at[i]).wait()
        sent.clear()

    mult = pl.multiple_of
    my_tok = pl.ds(mult(c * H, 16), H)
    other_tok = pl.ds(mult(oc * H, 16), H)
    my_rows = pl.ds(mult(y * B, 16), B)
    my_cols = pl.ds(mult(px * Q, 128), Q)
    mine = px * 4 + y
    nc = len(CHUNKS)

    bar = pltpu.get_barrier_semaphore()
    copies = [(fh_h, fh)]
    for lo, size in CHUNKS:
        copies.append((emb.at[pl.ds(mult(px * 768 + lo, 128), size), :], ew.at[pl.ds(lo, size), :]))
    copies += [(x_h.at[0], xv), (gains_h, gv), (tgt_h, tv)]
    for i in range(4):
        copies.append((emb.at[pl.ds(768 * i, W), my_cols], ec.at[pl.ds(W * i, W), :]))
    loads = [pltpu.make_async_copy(src, dst, lsem.at[i]) for i, (src, dst) in enumerate(copies)]
    early, late = loads[: 1 + nc], loads[1 + nc :]
    for cp in early:
        cp.start()
    for dev in plane[1:] + ring[1:] + group[1::2]:
        pl.semaphore_signal(bar, inc=1, device_id=dev, device_id_type=MESH)
    for cp in late:
        cp.start()

    loads[0].wait()
    sy = sems(nc)
    for n, (lo, size) in enumerate(CHUNKS):
        lanes = pl.ds(lo, size)
        loads[1 + n].wait()
        lp[:, lanes] = lax.dot_general(
            fh[...], ew[lanes, :], (((1,), (1,)), ((), ())), preferred_element_type=f32
        )
        if n == 0:
            pl.semaphore_wait(bar, 26)
        for k in (1, 3, 2):
            send(lp.at[pl.ds(mult(ys_at[k] * B, 16), B), lanes], ly.at[k - 1, :, lanes], sy + n, plane[k])

    late[0].wait()
    late[1].wait()
    late[2].wait()
    gb[...] = jnp.broadcast_to(gv[...], (8, C))
    sx = sems(2)
    for k in range(1, 4):
        cols = pl.ds(mult(xs_at[k] * Q, 128), Q)
        send(xv.at[my_tok, cols], xs.at[px], sx, plane[4 * k])
        send(gb.at[:, cols], gs.at[px], sx + 1, plane[4 * k])
    xf = xv[my_tok, :].astype(f32)
    xt[...] = to_rows([rsum(xf), rsum(xf * xf)], 8)
    xsl[mine] = xt[...]
    s1 = sems(1)
    for dev in plane[1:]:
        send(xt, xsl.at[mine], s1, dev)
    xs[px] = xv[my_tok, my_cols]
    gs[px] = gb[:, my_cols]
    tcol[...] = rsum(
        jnp.where(iota((T, T), 0) == iota((T, T), 1), tv[...].astype(f32), 0.0)
    ).astype(jnp.int32)

    sz = sems(nc)
    for n, (lo, size) in enumerate(CHUNKS):
        lanes = pl.ds(lo, size)
        landed(ly.at[:, :, lanes], sy + n)
        zl_buf[:, lanes] = lp[my_rows, lanes] + ly[0, :, lanes] + ly[1, :, lanes] + ly[2, :, lanes]
        send(zl_buf.at[:, lanes], zr_buf.at[:, lanes], sz + n, ring[4])

    landed(xsl.at[pl.ds(0, 15)], s1)
    rows = []
    for s in range(4):
        tot = xsl[4 * s] + xsl[4 * s + 1] + xsl[4 * s + 2] + xsl[4 * s + 3]
        rows += [tot[0:1], tot[1:2]]
    xz[0] = pick_rows(rows, 8)
    s2 = sems(1)
    send(xz.at[0], xz.at[1], s2, ring[4])
    landed(xs.at[pl.ds(0, 3)], sx)
    landed(gs.at[pl.ds(0, 3)], sx + 1)
    landed(xz.at[1], s2)
    tot = (xz[0] + xz[1]) * (1.0 / D)
    mu_rows, r_rows = [], []
    for s in range(4):
        mu = tot[2 * s : 2 * s + 1]
        mu_rows.append(mu)
        r_rows.append(lax.rsqrt(tot[2 * s + 1 : 2 * s + 2] - mu * mu + eps))
    rr[...] = pick_rows(r_rows, 8)
    cs[...] = to_cols(pick_rows(mu_rows + r_rows, 8))
    for s in range(4):
        xhs[s] = (xs[s].astype(f32) - cs[0:H, s : s + 1]) * cs[0:H, 4 + s : 5 + s]

    def gain(s):
        return gs[s][0:1, :]

    cols = []
    for j in range(1, 4):
        q1 = jnp.ones((H, Q), f32)
        q2 = xhs[j]
        for s in range(j - 1, -1, -1):
            a1 = q1 * gain(s)
            a2 = q2 * gain(s)
            xh = xhs[s]
            cols += [rsum(a1), rsum(a1 * xh), rsum(a2), rsum(a2 * xh)]
            if s > 0:
                r_col = cs[0:H, 4 + s : 5 + s]
                q1 = q1 + r_col * a1
                q2 = q2 + r_col * a2
    gt[...] = to_rows(cols, 24)
    sgx = sems(1)
    for k in range(1, 4):
        send(gt, gx.at[k - 1], sgx, plane[4 * k])

    first = [(base + lax.rem(y + k * oc, 4), lax.rem(px + k * c, 4), t) for k in range(4)]
    second = [(base + lax.rem(y + k * c, 4), lax.rem(px + k * oc, 4), t) for k in range(4)]

    def block(b, e_):
        return lax.rem(px - b * c - e_ * oc + 4, 4), lax.rem(y - b * oc - e_ * c + 4, 4)

    def pref(n, b):
        bx, by = block(b, 0)
        lo, size = CHUNKS[n]
        return pb.at[bx, pl.ds(mult(by * B, 16), B), pl.ds(lo, size)]

    a1 = sems(3 * nc)
    a2 = sems(4 * nc)

    def first_sends(n):
        own = pref(n, 0)
        for k in (1, 3, 2):
            send(own, own, a1 + 3 * n + k - 1, first[k])

    def second_sends(n, b):
        own = pref(n, b)
        for k in (1, 3, 2):
            send(own, own, a2 + 4 * n + b, second[k])

    def forward(n):
        for b in (1, 3, 2):
            landed(pref(n, b), a1 + 3 * n + b - 1)
            second_sends(n, b)

    first_lane = jnp.where(px == 0, 0, 128)
    tops, sums_, hits = [], [], []
    for n, (lo, size) in enumerate(CHUNKS):
        lanes = pl.ds(lo, size)
        landed(zr_buf.at[:, lanes], sz + n)
        lane = iota((B, size), 1) + lo
        valid = lane >= first_lane
        logits = jnp.where(valid, zl_buf[:, lanes] + zr_buf[:, lanes], LOW)
        m = jnp.max(logits, axis=1, keepdims=True)
        e = jnp.where(valid, jnp.exp(logits - m), 0.0)
        hit = (lane + (t * V + px * 768) == tcol[my_rows, :]) & valid
        pb[px, my_rows, lanes] = e.astype(bf16)
        first_sends(n)
        second_sends(n, 0)
        tops.append(m)
        sums_.append(rsum(e))
        hits.append(rsum(jnp.where(hit, logits, 0.0)))
        if n:
            forward(n - 1)

    top = functools.reduce(jnp.maximum, tops)
    total = sum(a * jnp.exp(b - top) for a, b in zip(sums_, tops))
    st[0] = to_rows([top, total, sum(hits)] + tops, 8)
    sst = sems(1)
    for k in range(1, 8):
        send(st.at[0], st.at[k], sst, group[k])

    landed(gx, sgx)
    gt2[...] = gt[...] + gx[0] + gx[1] + gx[2]
    sgy = sems(1)
    for k in range(1, 4):
        send(gt2, gy.at[k - 1], sgy, plane[k])

    forward(nc - 1)

    landed(st.at[pl.ds(1, 7)], sst)
    tiles = [st[k] for k in range(8)]
    top = functools.reduce(jnp.maximum, [a[0:1] for a in tiles])
    total = sum(a[1:2] * jnp.exp(a[0:1] - top) for a in tiles)
    st2[mine] = pick_rows(
        [top, total, sum(a[2:3] for a in tiles)] + [tiles[0][3 + n : 4 + n] for n in range(len(CHUNKS))], 8
    )
    s3 = sems(1)
    for dev in plane[1:]:
        send(st2.at[mine], st2.at[mine], s3, dev)

    landed(gy, sgy)
    gt3[...] = gt2[...] + gy[0] + gy[1] + gy[2]
    sgz = sems(1)
    send(gt3, gz, sgz, ring[4])
    landed(st2.at[pl.ds(0, 15)], s3)

    rows = []
    for yy in range(4):
        tiles = [st2[4 * xx + yy] for xx in range(4)]
        top = functools.reduce(jnp.maximum, [a[0:1] for a in tiles])
        total = sum(a[1:2] * jnp.exp(a[0:1] - top) for a in tiles)
        inv = 1.0 / total
        rows += [jnp.exp(a[3 + n : 4 + n] - top) * inv for a in tiles for n in range(4)]
        rows += [jnp.exp(sum(a[2:3] for a in tiles) - top) * inv - 1.0]
        rows += [None] * 15
    sc[...] = to_cols(pick_rows(rows, 128))

    def normalise(n, b, e_):
        bx, by = block(b, e_)
        lo, size = CHUNKS[n]
        lanes = pl.ds(lo, size)
        blk = pl.ds(mult(by * B, 16), B)
        pick = iota((B, 128), 1)
        scale = rsum(jnp.where(pick == by * 32 + bx * 4 + n, sc[0:B, :], 0.0))
        point = rsum(jnp.where(pick == by * 32 + 16, sc[0:B, :], 0.0))
        lane = iota((B, size), 1) + lo
        hit = (lane + (t * V + bx * 768) == tcol[blk, :]) & (lane >= jnp.where(bx == 0, 0, 128))
        pn[blk, pl.ds(mult(bx * W + lo, 128), size)] = jnp.where(hit, point, pb[bx, blk, lanes].astype(f32) * scale).astype(bf16)

    for n, (lo, size) in enumerate(CHUNKS):
        @pl.loop(0, 4)
        def _(b):
            normalise(n, b, 0)

        for b in (0, 1, 3, 2):
            landed(pb.at[0, pl.ds(0, 3 * B), pl.ds(lo, size)], a2 + 4 * n + b)

            @pl.loop(1, 4)
            def _(k):
                normalise(n, b, k)

    for cp in late[3:]:
        cp.wait()
    G[...] = jnp.dot(pn[...], ec[...], preferred_element_type=f32)

    sc0 = sems(1)
    send(G.at[other_tok, :], cr, sc0, twin)
    landed(gz, sgz)
    gram[...] = gt3[...] + gz[...]
    landed(cr, sc0)
    gh[...] = G[my_tok, :] + cr[...]
    szr = sems(1)
    for k in (1, 3, 2):
        send(gh.at[pl.ds(mult(zl_at[k] * R, 8), R), :], zrs.at[k - 1], szr, line[k])

    q = gh[...]
    cols = []
    for s in (3, 2, 1, 0):
        a = q * gain(s)
        cols += [rsum(a), rsum(a * xhs[s])]
        if s > 0:
            q = q + cs[0:H, 4 + s : 5 + s] * a
    sm[...] = to_rows(cols, 8)
    ssm = sems(1)
    for k in range(1, 8):
        send(sm, smz.at[k], ssm, ring[k])

    fcols = fh[:, my_cols]

    def head(windows):
        for i in windows:
            lo = 128 if i else 0
            res = lax.dot_general(
                pn[:, W * i + lo : W * (i + 1)], fcols, (((0,), (0,)), ((), ())), preferred_element_type=f32
            )
            hd[768 * i + lo : 768 * i + W, :] = res.astype(bf16)

    head((0,))
    landed(zrs, szr)
    mine24 = gh[pl.ds(mult(zl * R, 8), R), :] + zrs[0] + zrs[1] + zrs[2]
    ga[zl] = jnp.concatenate([mine24, jnp.zeros((8, Q), f32)], axis=0).astype(bf16)
    sga = sems(1)
    for k in (1, 3, 2):
        send(ga.at[zl], ga.at[zl], sga, line[k])

    landed(smz.at[pl.ds(1, 7)], ssm)
    sm2[...] = sm[...] + sum(smz[k] for k in range(1, 8))
    sxy = sems(1)
    for i in range(1, 16):
        send(sm2, smxy.at[i], sxy, plane[i])

    flush()
    head((1, 2, 3))
    landed(smxy.at[pl.ds(1, 15)], sxy)

    sums = (sm2[...] + sum(smxy[i] for i in range(1, 16))) * (1.0 / D)
    gram_m = gram[...] * (1.0 / D)
    at = {}
    for j in range(1, 4):
        for s in range(j - 1, -1, -1):
            at[j, s] = 4 * len(at)
    c1, c2 = {}, {}
    for n, s in enumerate((3, 2, 1, 0)):
        m1 = sums[2 * n : 2 * n + 1]
        m2 = sums[2 * n + 1 : 2 * n + 2]
        for j in range(s + 1, 4):
            o = at[j, s]
            m1 = m1 - c1[j] * gram_m[o : o + 1] - c2[j] * gram_m[o + 2 : o + 3]
            m2 = m2 - c1[j] * gram_m[o + 1 : o + 2] - c2[j] * gram_m[o + 3 : o + 4]
        c1[s] = rr[s : s + 1, :] * m1
        c2[s] = rr[s : s + 1, :] * m2
    coef = to_cols(pick_rows([c1[s] for s in range(4)] + [c2[s] for s in range(4)], 8))

    landed(ga.at[pl.ds(0, 3)], sga)
    for zz in range(4):
        g0f[R * zz : R * zz + R, :] = ga[zz].astype(f32)[0:R]
    h = g0f[...]
    for s in (3, 2, 1, 0):
        h = h + cs[0:H, 4 + s : 5 + s] * (h * gain(s)) - coef[0:H, s : s + 1] - coef[0:H, 4 + s : 5 + s] * xhs[s]
    g0s[my_tok, :] = h.astype(bf16)
    sc1 = sems(1)
    send(g0s.at[my_tok, :], g0s.at[my_tok, :], sc1, twin)
    landed(g0s.at[other_tok, :], sc1)
    g0b[...] = g0s[...]
    flush()


def add_rows(hd, g0, ids, out, res, osem):
    parts = [pl.ds(i * STEP, STEP) for i in range(V // STEP)]
    first = lax.axis_index("tensor") * V
    stores = []
    for i, p in enumerate(parts):
        rows = iota((STEP, T), 0) + (first + i * STEP)
        onehot = jnp.where(rows == ids[...], 1.0, 0.0).astype(bf16)
        added = jnp.dot(onehot, g0[...], preferred_element_type=f32).astype(bf16)
        res[p, :] = (hd[p, :].astype(f32) + added.astype(f32)).astype(bf16)
        stores.append(pltpu.make_async_copy(res.at[p, :], out.at[p, :], osem.at[i]))
        stores[-1].start()
    for cp in stores:
        cp.wait()


def local(emb, final_hidden, section_inputs, gains, token_ids, targets):
    hbm = pl.BlockSpec(memory_space=pltpu.HBM)
    vmem = pl.BlockSpec(memory_space=pltpu.VMEM)
    vm = lambda shape, dtype=f32: pltpu.VMEM(shape, dtype)
    tile = (8, 128)
    args = (emb, final_hidden, section_inputs, gains, targets.reshape(1, T))
    hd, g0 = pl.pallas_call(
        kernel,
        out_shape=(pltpu.VMEM((V, Q), bf16), pltpu.VMEM((T, Q), bf16)),
        in_specs=[hbm] * 5,
        out_specs=(vmem, vmem),
        scratch_shapes=[
            vm((W, C), bf16), vm((4 * W, Q), bf16), vm((T, C), bf16), vm((T, C), bf16),
            vm((1, C)), vm((1, T), jnp.int32), vm((T, 1), jnp.int32), vm((8, C)),
            vm((T, W)), vm((3, B, W)), vm((B, W)), vm((B, W)), vm((4, T, W), bf16), vm((T, 4 * W), bf16),
            vm((8,) + tile), vm((16,) + tile), vm((128, 128)),
            vm(tile), vm((16,) + tile), vm((2,) + tile), vm((4, H, Q), bf16), vm((4, 8, Q)),
            vm((128, 128)), vm(tile), vm((4, H, Q)),
            vm((24, 128)), vm((3, 24, 128)), vm((24, 128)), vm((3, 24, 128)),
            vm((24, 128)), vm((24, 128)), vm((24, 128)),
            vm((T, Q)), vm((H, Q)), vm((H, Q)), vm((3, R, Q)), vm((4, 32, Q), bf16),
            vm(tile), vm((8,) + tile), vm(tile), vm((16,) + tile), vm((H, Q)), vm((T, Q), bf16),
            pltpu.SemaphoreType.DMA((12,)),
            pltpu.SemaphoreType.DMA((N_SEM,)), pltpu.SemaphoreType.DMA((N_SEM,)),
        ],
        name="relay",
        compiler_params=pltpu.CompilerParams(
            collective_id=0, has_side_effects=True, vmem_limit_bytes=40 * 2**20
        ),
    )(*[pltpu.with_memory_space_constraint(a, pltpu.HBM) for a in args])
    return pl.pallas_call(
        add_rows,
        out_shape=jax.ShapeDtypeStruct((V, Q), bf16),
        in_specs=[vmem] * 3,
        out_specs=pl.BlockSpec(memory_space=pl.ANY),
        scratch_shapes=[vm((V, Q), bf16), pltpu.SemaphoreType.DMA((V // STEP,))],
        name="add_rows",
        compiler_params=pltpu.CompilerParams(vmem_limit_bytes=30 * 2**20),
    )(
        pltpu.with_memory_space_constraint(hd, pltpu.VMEM),
        pltpu.with_memory_space_constraint(g0, pltpu.VMEM),
        token_ids.reshape(1, T),
    )


def solution(mesh):
    placed = (P("tensor", "dp"), P(None, "dp"), P("pipe", None, "dp"), P("pipe", "dp"), P(), P())
    return jax.shard_map(
        local, mesh=mesh, in_specs=placed, out_specs=P("tensor", ("dp", "pipe")), check_vma=False
    )
```
